512 devices in a mesh: row: 64 (over y, x, core), col: 8 (over z).
Axes of the slice: x: 4, y: 8, z: 8, core: 2. Of those that a mesh axis runs over, the one named last changes fastest.
Arguments:
- panel_u: bfloat16 [64, 2560, 128], P('row'), may hold values from -0.125 to 0.125
- panel_v: bfloat16 [64, 2560, 128], P('row', 'col'), may hold values from -0.25 to 0.25
- linv: bfloat16 [2560, 2560], P('row', 'col')
- trail_u: bfloat16 [64, 16, 2560, 128], P('row', 'col'), may hold values from -0.125 to 0.125
- trail_v: bfloat16 [64, 16, 2560, 128], P('row', 'col'), may hold values from -0.125 to 0.125
- rank_map: int32 [64, 64], replicated, may hold values from 32 to 128, as said below
- tile_of_slot: int32 [64], replicated, may hold values from 0 to 63, each once
- band_cols: int32 [16], P('col'), may hold values from 0 to 63, as said below
Outputs:
- gram_left: float32 [64, 16, 256, 256], P('row', 'col')
- gram_right: float32 [64, 16, 256, 256], P('row', 'col')
The draws below stay inside these ranges and needn't reach their ends.
Inputs may be any that keep to these rules, and one draw needn't show every extreme that they name: rank_map[i, j] for j != i is the rank of trailing tile (i, j), including band tiles with j > i, whose core is zero; rank_map[i, i] is the rank of panel tile i; some panel tile has rank 128. `tile_of_slot`: a permutation. `band_cols`: distinct values.
All inputs are finite; a program needn't handle non-finite values.
Results may differ from the reference program's by a relative error of at most 0.0049.
Values may be sent and summed in bfloat16 or wider, within the bound.
A program may use at most 64 MiB of HBM per device.

```python
import math
import jax
import jax.numpy as jnp
from jax import lax

B = 2560
R = 128
NT = 64
NC = 16


def draw_linv(key, part):
    diag_key, off_key = jax.random.split(jax.random.fold_in(key, 11))
    row_ids = jnp.arange(B)[:, None]
    col_ids = jnp.arange(B)[None, :]
    diagonal = jax.random.uniform(diag_key, (B, B), jnp.float32, 0.5, 1.5)
    spread = jax.random.normal(off_key, (B, B), jnp.float32)
    lower = jnp.where(row_ids > col_ids, spread * (1.0 / math.sqrt(B)), 0.0)
    return jnp.where(row_ids == col_ids, diagonal, lower).astype(jnp.bfloat16)


def draw_rank_map(key, part):
    value_key, spot_key = jax.random.split(jax.random.fold_in(key, 23))
    ranks = jax.random.randint(value_key, (NT, NT), R // 4, R + 1)
    spot = jax.random.randint(spot_key, (), 0, NT)
    tile_ids = jnp.arange(NT)
    on_spot = (tile_ids[:, None] == spot) & (tile_ids[None, :] == spot)
    return jnp.where(on_spot, R, ranks).astype(jnp.int32)


def draw_band_cols(key, part):
    order = jax.random.permutation(jax.random.fold_in(key, 37), NT)
    return order[:NC].astype(jnp.int32)


def levels(stream_key, dims, cuts, least, high):
    factor_of, own = 1.0, jax.random.fold_in(stream_key, 6)
    for axis_at, shards_of in cuts:
        steps = jnp.exp(jax.random.uniform(jax.random.fold_in(own, axis_at), (shards_of,), jnp.float32, least / len(cuts), high / len(cuts)))
        factor_of = factor_of * jnp.repeat(steps, dims[axis_at] // shards_of).reshape([-1 if axis == axis_at else 1 for axis in range(len(dims))])
    return factor_of


def noise(key, shape, scale, most, cuts=(), kind=jnp.bfloat16):
    values = jax.random.normal(key, shape, jnp.float32) * scale
    if len(cuts) > 0:
        values = levels(key, shape, cuts, -0.22, 0.18) * values
    return jnp.clip(values, min=-most, max=most).astype(kind)


def setup_inputs(seed: int = 0) -> dict:
    streams_of = jax.random.split(jax.random.key(seed), 9)
    return {
        "panel_u": noise(streams_of[0], (NT, B, R), B ** -0.5, 0.125, ((0, 64),)),
        "panel_v": noise(streams_of[1], (NT, B, R), ((B * R) ** 0.5) ** -0.5, 0.25, ((0, 64), (1, 8))),
        "linv": draw_linv(jax.random.fold_in(streams_of[8], 71), 0),
        "trail_u": noise(streams_of[3], (NT, NC, B, R), B ** -0.5, 0.125, ((0, 64), (1, 8))),
        "trail_v": noise(streams_of[4], (NT, NC, B, R), B ** -0.5, 0.125, ((0, 64), (1, 8))),
        "rank_map": draw_rank_map(jax.random.fold_in(streams_of[8], 71), 0),
        "tile_of_slot": jax.random.permutation(streams_of[6], NT).astype(jnp.int32),
        "band_cols": draw_band_cols(jax.random.fold_in(streams_of[8], 71), 0),
    }


def reference(panel_u, panel_v, linv, trail_u, trail_v, rank_map, tile_of_slot, band_cols):
    columns = jnp.arange(R, dtype=jnp.int32)
    slot_ids = jnp.arange(NT, dtype=jnp.int32)
    diag_rank = jnp.sum(jnp.where(slot_ids[:, None] == slot_ids[None, :], rank_map, 0), axis=1)
    slot_rank = jnp.sum(jnp.where(tile_of_slot[:, None] == slot_ids[None, :], diag_rank[None, :], 0), axis=1)
    kept_cols = columns[None, None, :] < slot_rank[:, None, None]
    masked_u = jnp.where(kept_cols, panel_u, jnp.zeros_like(panel_u))
    masked_v = jnp.where(kept_cols, panel_v, jnp.zeros_like(panel_v))

    def solve_factor(factor):
        return jnp.dot(linv, factor, preferred_element_type=jnp.float32).astype(jnp.bfloat16)

    solved = lax.map(solve_factor, masked_v)
    slot_of_tile = jnp.sum(jnp.where(tile_of_slot[None, :] == slot_ids[:, None], slot_ids[None, :], 0), axis=1)

    def one_tile(tile_pair):
        slot_now = tile_pair[0]
        band_now = tile_pair[1]
        own_tile = tile_of_slot[slot_now]
        band_tile = band_cols[band_now]
        source = slot_of_tile[band_tile]
        core_mat = jnp.dot(solved[slot_now].T, solved[source], preferred_element_type=jnp.float32)
        core_mat = jnp.where(band_tile < own_tile, core_mat, jnp.zeros_like(core_mat)).astype(jnp.bfloat16)
        update = jnp.dot(masked_u[source], core_mat.T, preferred_element_type=jnp.float32).astype(jnp.bfloat16)
        trail_keep = columns[None, :] < rank_map[own_tile, band_tile]
        kept_u = jnp.where(trail_keep, trail_u[slot_now, band_now], jnp.zeros_like(update))
        kept_v = jnp.where(trail_keep, trail_v[slot_now, band_now], jnp.zeros_like(update))
        left_stack = jnp.concatenate([kept_u, masked_u[slot_now]], axis=1)
        right_stack = jnp.concatenate([kept_v, -update], axis=1)
        left_gram = jnp.dot(left_stack.T, left_stack, preferred_element_type=jnp.float32)
        right_gram = jnp.dot(right_stack.T, right_stack, preferred_element_type=jnp.float32)
        return left_gram, right_gram

    slot_grid = jnp.repeat(slot_ids, NC)
    band_grid = jnp.tile(jnp.arange(NC, dtype=jnp.int32), NT)
    tile_pairs = jnp.stack([slot_grid, band_grid], axis=1).astype(jnp.int32)
    left_grams, right_grams = lax.map(one_tile, tile_pairs)
    return left_grams.reshape(NT, NC, 2 * R, 2 * R), right_grams.reshape(NT, NC, 2 * R, 2 * R)
```

```python
import functools

import jax
import jax.numpy as jnp
from jax import lax
from jax.experimental import pallas as pl
from jax.experimental.pallas import tpu as pltpu
from jax.sharding import PartitionSpec as P

MESH = pl.DeviceIdType.MESH
BF = jnp.bfloat16
F32 = jnp.float32
HI = lax.Precision.HIGHEST


def near_first(n):
    return sorted(range(1, n), key=lambda d: (min(d, n - d), d))


def cross_rows(first, second):
    return lax.dot_general(first, second, (((0,), (0,)), ((), ())), preferred_element_type=F32)


def flag_row(shape_like, cond):
    return jnp.where(cond, jnp.ones(shape_like, F32), jnp.zeros(shape_like, F32))


def plan(ny, nx, nz):
    counts = dict(
        v=1, usib=1, bc=nz, ly=ny, lx=ny * nx, zs=nz, ub=nx, uc=ny, ud=ny, ue=nx, uf=1,
        yx=nx, yy=ny, yg=ny, yh=nx, pc=nz, zc=nz,
    )
    base, total = {}, 0
    for name, count in counts.items():
        base[name] = total
        total += count
    return base, total


def kernel(
    dims,
    panel_u, panel_v, linv, trail_u, trail_v, rank_map, tile_of_slot, band_cols, band_rows,
    gram_left, gram_right,
    basis, basis_sib, chosen, ux, ured, uy, upiece, uband, tu, tv,
    vchip, lbuf, zsend, zrecv, sol, selx, bsel, yrecv, yred, yg, bcbuf,
    pown, psend, psib, csend, crecv, right,
    ssem, rsem, lsem,
):
    ny, nx, nz = dims
    base, _ = plan(ny, nx, nz)
    points, rank = basis.shape
    depth = linv.shape[0]
    row = lax.axis_index("row")
    z = lax.axis_index("col")
    y, x, h = row // (2 * nx), (row // 2) % nx, row % 2
    sib = 1 - h
    spot = lambda yy, xx, hh: (yy * nx + xx) * 2 + hh

    def to_y(d):
        return {"row": spot((y + d) % ny, x, h), "col": z}

    def to_x(d):
        return {"row": spot(y, (x + d) % nx, h), "col": z}

    def to_z(d):
        return {"row": row, "col": (z + d) % nz}

    to_sib = {"row": spot(y, x, sib), "col": z}

    def copy(src, dst, name, k, where, rk=None):
        return pltpu.make_async_remote_copy(
            src_ref=src, dst_ref=dst,
            send_sem=ssem.at[base[name] + k],
            recv_sem=rsem.at[base[name] + (k if rk is None else rk)],
            device_id=where, device_id_type=MESH,
        )

    barrier = pltpu.get_barrier_semaphore()
    peers = [to_y(d) for d in near_first(ny)] + [to_x(d) for d in near_first(nx)]
    peers += [to_z(d) for d in near_first(nz)] + [to_sib]
    for peer in peers:
        pl.semaphore_signal(barrier, inc=1, device_id=peer, device_id_type=MESH)

    load_u = pltpu.make_async_copy(trail_u.at[0], tu, lsem.at[0])
    load_v = pltpu.make_async_copy(trail_v.at[0], tv, lsem.at[1])
    load_u.start()
    load_v.start()

    lanes = lax.broadcasted_iota(jnp.int32, (1, rank), 1)
    own_tile = tile_of_slot[row]
    own_mask = flag_row((1, rank), lanes < rank_map[own_tile, own_tile]).astype(BF)
    mine = pl.multiple_of(h * rank, rank)
    vchip[:, pl.ds(mine, rank)] = panel_v[0] * own_mask
    lbuf[y, x] = linv[...]
    bcbuf[z] = band_rows[...]
    step = points // 4
    for k in range(4):
        basis[k * step:(k + 1) * step, :] = panel_u[0, k * step:(k + 1) * step, :] * own_mask

    pl.semaphore_wait(barrier, len(peers))

    waits = []
    cv = copy(vchip.at[:, pl.ds(mine, rank)], vchip.at[:, pl.ds(mine, rank)], "v", 0, to_sib)
    cv.start()
    waits.append(cv)
    ly = {}
    for d in near_first(ny):
        ly[d] = copy(linv, lbuf.at[y, x], "ly", d, to_y(d))
        ly[d].start()
    bcs = {}
    for d in near_first(nz):
        bcs[d] = copy(band_rows, bcbuf.at[z], "bc", d, to_z(d))
        bcs[d].start()
    cu = copy(basis, basis_sib, "usib", 0, to_sib)
    cu.start()

    lx = {}

    def forward(d):
        yy = (y - d) % ny
        src = linv if d == 0 else lbuf.at[yy, x]
        for dx in near_first(nx):
            lx[d, dx] = copy(src, lbuf.at[yy, x], "lx", d * nx + dx, to_x(dx))
            lx[d, dx].start()

    order_y = [0] + near_first(ny)
    forward(0)
    for d in near_first(ny):
        ly[d].wait_recv()
        forward(d)

    cu.wait_recv()
    band_tile = band_cols[h]
    f_own = flag_row((1, rank), jnp.broadcast_to(own_tile == band_tile, (1, rank))).astype(BF)
    sib_tile = tile_of_slot[spot(y, x, sib)]
    f_sib = flag_row((1, rank), jnp.broadcast_to(sib_tile == band_tile, (1, rank))).astype(BF)
    px = points // nx
    for k in range(nx):
        part = slice(k * px, (k + 1) * px)
        chosen[k] = basis[part, :] * f_own + basis_sib[part, :] * f_sib
    ub = {}
    for d in near_first(nx):
        ub[d] = copy(chosen.at[(x + d) % nx], ux.at[x], "ub", d, to_x(d))
        ub[d].start()

    cv.wait_recv()
    zs = {}
    for d in order_y:
        yy = (y - d) % ny
        for dx in near_first(nx):
            lx[d, dx].wait_recv()
        block = lbuf[yy].astype(F32).reshape(nx * depth, linv.shape[1]).astype(BF)
        part = jnp.dot(block, vchip[...], preferred_element_type=F32)
        part = part.reshape(nx, depth, 2 * rank).astype(BF)
        zsend[d] = part
        e = (yy + nz - z) % nz
        zs[d] = copy(zsend.at[d], zrecv.at[z], "zs", d, {"row": row, "col": yy}, rk=e)

        @pl.when(e != 0)
        def _():
            zs[d].start()

        @pl.when(e == 0)
        def _():
            zrecv[z] = part

    for d in near_first(nx):
        ub[d].wait_recv()
    total = chosen[x]
    for d in range(1, nx):
        total = total + ux[(x + d) % nx]
    py = px // ny
    ured[...] = total.reshape(ny, py, rank)
    uc = {}
    for d in near_first(ny):
        uc[d] = copy(ured.at[(y + d) % ny], uy.at[y], "uc", d, to_y(d))
        uc[d].start()

    load_u.wait()
    chunk = points // 5
    keeps = [
        flag_row((1, rank), lanes < rank_map[own_tile, band_cols[i]]).astype(BF) for i in range(2)
    ]

    def left_gram(i):
        gram_left[0, i] = jnp.zeros((2 * rank, 2 * rank), F32)

        def body(k, carry):
            rows = pl.ds(pl.multiple_of(k * chunk, 16), chunk)
            both = jnp.concatenate([tu[i, rows, :] * keeps[i], basis[rows, :]], axis=1)
            gram_left[0, i] += cross_rows(both, both)
            return carry

        lax.fori_loop(0, 5, body, 0)

    left_gram(0)

    for d in near_first(ny):
        uc[d].wait_recv()
    total = ured[y]
    for d in range(1, ny):
        total = total + uy[(y + d) % ny]
    my_piece = pl.ds(pl.multiple_of((x * ny + y) * py, 16), py)
    my_slab = pl.ds(pl.multiple_of(x * px, 16), px)
    upiece[...] = total
    uband[h, my_piece, :] = total
    ud = {}
    for d in near_first(ny):
        ud[d] = copy(upiece, uband.at[h, my_piece, :], "ud", d, to_y(d))
        ud[d].start()

    for e in range(1, nz):
        copy(zsend.at[0], zrecv.at[z], "zs", 0, to_z(1), rk=e).wait_recv()
    acc = zrecv[0].astype(F32)
    for k in range(1, nz):
        acc = acc + zrecv[k].astype(F32)
    sol[...] = acc.astype(BF)
    yx = {}
    for d in near_first(nx):
        yx[d] = copy(sol.at[(x + d) % nx], selx.at[x], "yx", d, to_x(d))
        yx[d].start()
    selx[x] = sol[x]

    for d in near_first(ny):
        ud[d].wait_recv()
    ue = {}
    for d in near_first(nx):
        ue[d] = copy(uband.at[h, my_slab, :], uband.at[h, my_slab, :], "ue", d, to_x(d))
        ue[d].start()

    for d in near_first(nz):
        bcs[d].wait_recv()
    for d in near_first(nx):
        yx[d].wait_recv()
    tiles = [tile_of_slot[spot(y, k // 2, k % 2)] for k in range(2 * nx)]
    blocks = [
        selx[k // 2, :, (k % 2) * rank:(k % 2 + 1) * rank].astype(F32) for k in range(2 * nx)
    ]
    for p in range(nz):
        for i in range(2):
            name_row = bcbuf[p][i:i + 1, :]
            got = jnp.zeros((depth, rank), F32)
            for k in range(2 * nx):
                got = got + blocks[k] * flag_row((1, rank), name_row == tiles[k])
            bsel[p, :, i * rank:(i + 1) * rank] = got.astype(BF)
    yy_copies = {}
    for d in near_first(ny):
        yy_copies[d] = copy(bsel.at[(y + d) % ny], yrecv.at[y], "yy", d, to_y(d))
        yy_copies[d].start()
    yrecv[y] = bsel[y]
    for d in near_first(ny):
        yy_copies[d].wait_recv()
    acc = yrecv[0].astype(F32)
    for k in range(1, ny):
        acc = acc + yrecv[k].astype(F32)
    yred[...] = acc.astype(BF)
    yg[x, y] = acc.astype(BF)
    ygc = {}
    for d in near_first(ny):
        ygc[d] = copy(yred, yg.at[x, y], "yg", d, to_y(d))
        ygc[d].start()

    for d in near_first(nx):
        ue[d].wait_recv()
    uf = copy(uband.at[h], uband.at[h], "uf", 0, to_sib)
    uf.start()

    for d in near_first(ny):
        ygc[d].wait_recv()
    yh = {}
    for d in near_first(nx):
        yh[d] = copy(yg.at[x], yg.at[x], "yh", d, to_x(d))
        yh[d].start()

    left_gram(1)
    load_v.wait()
    uf.wait_recv()

    def right_gram(i):
        right[i] = jnp.zeros((2 * rank, 2 * rank), F32)

        def body(k, carry):
            rows = pl.ds(pl.multiple_of(k * chunk, 16), chunk)
            both = jnp.concatenate([tv[i, rows, :] * keeps[i], uband[i, rows, :]], axis=1)
            right[i] += cross_rows(both, both)
            return carry

        lax.fori_loop(0, 5, body, 0)

    right_gram(0)

    for d in near_first(nx):
        yh[d].wait_recv()
    sol_rows = sol[...].astype(F32).reshape(nx * depth, 2 * rank).astype(BF)
    order_z = near_first(nz) + [0]
    pcs = {}
    for e in order_z:
        p = (z + e) % nz
        y_rows = jnp.concatenate([yg[k, p].astype(F32) for k in range(nx)], axis=0).astype(BF)
        part = cross_rows(sol_rows, y_rows)
        low, high = part[:rank], part[rank:]
        pown[e] = jnp.where(h == 0, low, high)
        psend[e] = jnp.where(h == 0, high, low)
        pcs[e] = copy(psend.at[e], psib.at[e], "pc", e, to_sib)
        pcs[e].start()
    zc = {}
    for e in order_z:
        pcs[e].wait_recv()
        csum = (pown[e] + psib[e]).astype(BF)
        if e == 0:
            crecv[z] = csum
        else:
            csend[e] = csum
            zc[e] = copy(csend.at[e], crecv.at[z], "zc", e, to_z(e))
            zc[e].start()

    right_gram(1)

    for e in near_first(nz):
        zc[e].wait_recv()
    core = crecv[0].astype(F32)
    for k in range(1, nz):
        core = core + crecv[k].astype(F32)
    for i in range(2):
        lower = flag_row((1, rank), jnp.broadcast_to(band_cols[i] < own_tile, (1, rank)))
        c = (core[:, i * rank:(i + 1) * rank] * lower).astype(BF).astype(F32)
        g = right[i, :rank, rank:]
        gram_uu = right[i, rank:, rank:]
        cross = -lax.dot_general(g, c, (((1,), (1,)), ((), ())), precision=HI, preferred_element_type=F32)
        crossed = -lax.dot_general(c, g, (((1,), (1,)), ((), ())), precision=HI, preferred_element_type=F32)
        half = jnp.dot(c, gram_uu, precision=HI, preferred_element_type=F32)
        corner = lax.dot_general(half, c, (((1,), (1,)), ((), ())), precision=HI, preferred_element_type=F32)
        gram_right[0, i, :rank, :rank] = right[i, :rank, :rank]
        gram_right[0, i, :rank, rank:] = cross
        gram_right[0, i, rank:, :rank] = crossed
        gram_right[0, i, rank:, rank:] = corner

    for group in (ly, bcs, lx, ub, uc, ud, yx, ue, yy_copies, ygc, yh, pcs, zc):
        for one in group.values():
            one.wait_send()
    for one in (cv, cu, uf):
        one.wait_send()
    for d in order_y:
        yy = (y - d) % ny

        @pl.when((yy + nz - z) % nz != 0)
        def _():
            zs[d].wait_send()


def shards(dims, panel_u, panel_v, linv, trail_u, trail_v, rank_map, tile_of_slot, band_cols):
    ny, nx, nz = dims
    points, rank = panel_u.shape[1:]
    depth, width = linv.shape
    px = points // nx
    py = px // ny
    _, total = plan(ny, nx, nz)
    band_rows = jnp.broadcast_to(jnp.tile(band_cols, 4)[:, None], (8, rank))
    vmem = pl.BlockSpec(memory_space=pltpu.VMEM)
    smem = pl.BlockSpec(memory_space=pltpu.SMEM)
    hbm = pl.BlockSpec(memory_space=pl.ANY)
    out = jax.ShapeDtypeStruct((1, 2, 2 * rank, 2 * rank), F32)
    scratch = [
        pltpu.VMEM((points, rank), BF),
        pltpu.VMEM((points, rank), BF),
        pltpu.VMEM((nx, px, rank), BF),
        pltpu.VMEM((nx, px, rank), BF),
        pltpu.VMEM((ny, py, rank), BF),
        pltpu.VMEM((ny, py, rank), BF),
        pltpu.VMEM((py, rank), BF),
        pltpu.VMEM((2, points, rank), BF),
        pltpu.VMEM((2, points, rank), BF),
        pltpu.VMEM((2, points, rank), BF),
        pltpu.VMEM((width, 2 * rank), BF),
        pltpu.VMEM((ny, nx, depth, width), BF),
        pltpu.VMEM((ny, nx, depth, 2 * rank), BF),
        pltpu.VMEM((nz, nx, depth, 2 * rank), BF),
        pltpu.VMEM((nx, depth, 2 * rank), BF),
        pltpu.VMEM((nx, depth, 2 * rank), BF),
        pltpu.VMEM((nz, depth, 2 * rank), BF),
        pltpu.VMEM((ny, depth, 2 * rank), BF),
        pltpu.VMEM((depth, 2 * rank), BF),
        pltpu.VMEM((nx, nz, depth, 2 * rank), BF),
        pltpu.VMEM((nz, 8, rank), jnp.int32),
        pltpu.VMEM((nz, rank, 2 * rank), F32),
        pltpu.VMEM((nz, rank, 2 * rank), F32),
        pltpu.VMEM((nz, rank, 2 * rank), F32),
        pltpu.VMEM((nz, rank, 2 * rank), BF),
        pltpu.VMEM((nz, rank, 2 * rank), BF),
        pltpu.VMEM((2, 2 * rank, 2 * rank), F32),
        pltpu.SemaphoreType.DMA((total,)),
        pltpu.SemaphoreType.DMA((total,)),
        pltpu.SemaphoreType.DMA((2,)),
    ]
    return pl.pallas_call(
        functools.partial(kernel, dims),
        out_shape=(out, out),
        in_specs=[vmem, vmem, vmem, hbm, hbm, smem, smem, smem, vmem],
        out_specs=(vmem, vmem),
        scratch_shapes=scratch,
        compiler_params=pltpu.CompilerParams(
            collective_id=0, has_side_effects=True, vmem_limit_bytes=48 * 2**20
        ),
    )(panel_u, panel_v, linv, trail_u, trail_v, rank_map, tile_of_slot, band_cols, band_rows)


def solution(mesh):
    nz = mesh.shape["col"]
    ny = nz
    nx = mesh.shape["row"] // (2 * ny)
    return jax.shard_map(
        functools.partial(shards, (ny, nx, nz)),
        mesh=mesh,
        in_specs=(
            P("row", None, None),
            P("row", "col", None),
            P("row", "col"),
            P("row", "col", None, None),
            P("row", "col", None, None),
            P(),
            P(),
            P("col"),
        ),
        out_specs=(P("row", "col", None, None), P("row", "col", None, None)),
        check_vma=False,
    )
```

```python
import functools

import jax
import jax.numpy as jnp
from jax import lax
from jax.experimental import pallas as pl
from jax.experimental.pallas import tpu as pltpu
from jax.sharding import PartitionSpec as P

MESH = pl.DeviceIdType.MESH
BF = jnp.bfloat16
F32 = jnp.float32
HI = lax.Precision.HIGHEST


def near_first(n):
    return sorted(range(1, n), key=lambda d: (min(d, n - d), d))


def cross_rows(first, second):
    return lax.dot_general(first, second, (((0,), (0,)), ((), ())), preferred_element_type=F32)


def flag_row(shape_like, cond):
    return jnp.where(cond, jnp.ones(shape_like, F32), jnp.zeros(shape_like, F32))


def plan(ny, nx, nz):
    counts = dict(
        va=2 * nx, ua=2 * nx, vb=ny, ub=ny, vc=2 * nx, bc=nz, v=1, ly=ny, lx=ny * nx, zs=nz, zy=nz,
        gy=ny, gx=ny * nx, ut=1, ud=ny, ue=nx, uf=1, pc=ny, zc=nz,
    )
    base, total = {}, 0
    for name, count in counts.items():
        base[name] = total
        total += count
    return base, total


def kernel(
    dims,
    panel_u, panel_v, linv, trail_u, trail_v, rank_map, tile_of_slot, band_cols,
    gram_left, gram_right,
    basis, vown, vchip, vx, vsel, vy, vpiece, vband, ux, usel, uy, upiece, uband, tu, tv,
    lbuf, zsend, zrecv, sol, zysend, zyrecv, yg, bcbuf,
    pown, psend, psib, csend, crecv, right,
    ssem, rsem, lsem,
):
    ny, nx, nz = dims
    base, _ = plan(ny, nx, nz)
    points, rank = panel_u.shape[1:]
    depth, width = linv.shape
    py = width // nx
    row = lax.axis_index("row")
    z = lax.axis_index("col")
    y, x, h = row // (2 * nx), (row // 2) % nx, row % 2

    def spot(yy, xx, hh):
        return (yy * nx + xx) * 2 + hh

    def to_y(d):
        return {"row": spot((y + d) % ny, x, h), "col": z}

    def to_x(d, flip=0):
        return {"row": spot(y, (x + d) % nx, (h + flip) % 2), "col": z}

    def to_z(d):
        return {"row": row, "col": (z + d) % nz}

    to_sib = to_x(0, 1)
    to_turned = {"row": spot(z, x, h), "col": y}
    chips = [(0, 1)] + [(d, flip) for d in near_first(nx) for flip in (0, 1)]
    started = []

    def copy(src, dst, name, k, where, rk=None):
        return pltpu.make_async_remote_copy(
            src_ref=src, dst_ref=dst,
            send_sem=ssem.at[base[name] + k],
            recv_sem=rsem.at[base[name] + (k if rk is None else rk)],
            device_id=where, device_id_type=MESH,
        )

    def go(src, dst, name, k, where):
        one = copy(src, dst, name, k, where)
        one.start()
        started.append(one)
        return one

    def load(src, dst, k):
        one = pltpu.make_async_copy(src, dst, lsem.at[k])
        one.start()
        return one

    load_pv = load(panel_v.at[0], vown, 0)
    load_l = load(linv, lbuf.at[y, x], 1)
    load_pu = load(panel_u.at[0], basis, 2)

    barrier = pltpu.get_barrier_semaphore()
    peers = [to_y(d) for d in near_first(ny)] + [to_x(d, flip) for d, flip in chips]
    peers += [to_z(d) for d in near_first(nz)]
    for peer in peers:
        pl.semaphore_signal(barrier, inc=1, device_id=peer, device_id_type=MESH)

    @pl.when(y != z)
    def _():
        pl.semaphore_signal(barrier, inc=1, device_id=to_turned, device_id_type=MESH)

    load_tu = load(trail_u.at[0], tu, 3)
    load_tv = load(trail_v.at[0], tv, 4)

    lanes = lax.broadcasted_iota(jnp.int32, (1, rank), 1)
    own_tile = tile_of_slot[row]
    own_mask = flag_row((1, rank), lanes < rank_map[own_tile, own_tile]).astype(BF)
    mine = pl.multiple_of(h * rank, rank)
    odd = lax.broadcasted_iota(jnp.int32, (8, rank), 0) % 2
    bcbuf[z] = jnp.where(odd == 1, band_cols[1], band_cols[0])
    load_pv.wait()
    masked_v = vown[...] * own_mask
    vown[...] = masked_v
    vchip[:, pl.ds(mine, rank)] = masked_v
    load_pu.wait()
    step = points // 4
    for k in range(4):
        part = slice(k * step, (k + 1) * step)
        basis[part, :] = basis[part, :] * own_mask
    load_l.wait()

    pl.semaphore_wait(barrier, len(peers) + jnp.where(y != z, 1, 0))

    def quarter(k):
        return pl.ds(pl.multiple_of(k * py, 16), py)

    def uquarter(k):
        return pl.ds(pl.multiple_of(z * width + k * py, 16), py)

    va, ua, ly, bcs = {}, {}, {}, {}
    for d, flip in chips:
        xx = (x + d) % nx
        va[d, flip] = go(vown.at[quarter(xx), :], vx.at[x, h], "va", 2 * d + flip, to_x(d, flip))
    for d in near_first(nz):
        bcs[d] = go(bcbuf.at[z], bcbuf.at[z], "bc", d, to_z(d))
    for d in near_first(ny):
        ly[d] = go(lbuf.at[y, x], lbuf.at[y, x], "ly", d, to_y(d))
    cv = go(vchip.at[:, pl.ds(mine, rank)], vchip.at[:, pl.ds(mine, rank)], "v", 0, to_sib)
    for d, flip in chips:
        xx = (x + d) % nx
        ua[d, flip] = go(basis.at[uquarter(xx), :], ux.at[x, h], "ua", 2 * d + flip, to_x(d, flip))
    vx[x, h] = vown[quarter(x), :]
    ux[x, h] = basis[uquarter(x), :]

    lx = {}

    def forward_l(d):
        yy = (y - d) % ny
        for dx in near_first(nx):
            lx[d, dx] = go(lbuf.at[yy, x], lbuf.at[yy, x], "lx", d * nx + dx, to_x(dx))

    order_y = [0] + near_first(ny)
    forward_l(0)

    def pick(from_ref, to_ref):
        blocks = [from_ref[k // 2, k % 2] for k in range(2 * nx)]
        for p in range(nz):
            name_row = bcbuf[p, pl.ds(h, 1), :]
            got = jnp.zeros((py, rank), BF)
            for k in range(2 * nx):
                got = got + blocks[k] * flag_row((1, rank), name_row == tiles[k]).astype(BF)
            to_ref[p] = got

    def summed(ref, count):
        total = ref[0]
        for k in range(1, count):
            total = total + ref[k]
        return total

    tiles = [tile_of_slot[spot(y, k // 2, k % 2)] for k in range(2 * nx)]
    for d in near_first(nz):
        bcs[d].wait_recv()
    for one in va.values():
        one.wait_recv()
    pick(vx, vsel)
    vb = {}
    for d in near_first(ny):
        vb[d] = go(vsel.at[(y + d) % ny], vy.at[y], "vb", d, to_y(d))
    vy[y] = vsel[y]

    for d in near_first(ny):
        ly[d].wait_recv()
        forward_l(d)

    for d in near_first(ny):
        vb[d].wait_recv()
    piece = summed(vy, ny)
    vpiece[...] = piece
    vband[x, :, pl.ds(mine, rank)] = piece
    vc = {}
    for d, flip in chips:
        vc[d, flip] = go(
            vpiece, vband.at[x, :, pl.ds(mine, rank)], "vc", 2 * d + flip, to_x(d, flip)
        )

    for one in ua.values():
        one.wait_recv()
    pick(ux, usel)
    ub = {}
    for d in near_first(ny):
        ub[d] = go(usel.at[(y + d) % ny], uy.at[y], "ub", d, to_y(d))
    uy[y] = usel[y]

    for one in vc.values():
        one.wait_recv()
    rows = jnp.concatenate([lbuf[k, x].astype(F32) for k in range(ny)], axis=0).astype(BF)
    part = jnp.dot(rows, vband[...].reshape(width, 2 * rank), preferred_element_type=F32)
    zysend[...] = part.reshape(ny, depth, 2 * rank).astype(BF)
    zy = {}
    for e in near_first(nz):
        zy[e] = go(zysend.at[(z + e) % nz], zyrecv.at[z], "zy", e, to_z(e))
    zyrecv[z] = zysend[z]

    for d in near_first(ny):
        ub[d].wait_recv()
    piece = summed(uy, ny)
    upiece[...] = piece
    ut = copy(upiece, uband.at[h, z, x], "ut", 0, to_turned)

    @pl.when(y != z)
    def _():
        ut.start()

    @pl.when(y == z)
    def _():
        uband[h, z, x] = piece

    cv.wait_recv()
    zs = {}
    for d in order_y:
        yy = (y - d) % ny
        for dx in near_first(nx):
            lx[d, dx].wait_recv()
        block = lbuf[yy].astype(F32).reshape(nx * depth, width).astype(BF)
        part = jnp.dot(block, vchip[...], preferred_element_type=F32)
        part = part.reshape(nx, depth, 2 * rank).astype(BF)
        zsend[d] = part
        e = (yy + nz - z) % nz
        zs[d] = copy(zsend.at[d], zrecv.at[z], "zs", d, {"row": row, "col": yy}, rk=e)

        @pl.when(e != 0)
        def _():
            zs[d].start()

        @pl.when(e == 0)
        def _():
            zrecv[z] = part

    @pl.when(y != z)
    def _():
        ut.wait_recv()

    ud = {}
    for d in near_first(ny):
        ud[d] = go(uband.at[h, y, x], uband.at[h, y, x], "ud", d, to_y(d))

    for e in near_first(nz):
        zy[e].wait_recv()
    acc = zyrecv[0].astype(F32)
    for k in range(1, nz):
        acc = acc + zyrecv[k].astype(F32)
    yg[x, y] = acc.astype(BF)
    gy, gx = {}, {}
    for d in near_first(ny):
        gy[d] = go(yg.at[x, y], yg.at[x, y], "gy", d, to_y(d))

    def forward_g(d):
        yy = (y - d) % ny
        for dx in near_first(nx):
            gx[d, dx] = go(yg.at[x, yy], yg.at[x, yy], "gx", d * nx + dx, to_x(dx))

    forward_g(0)
    for d in near_first(ny):
        gy[d].wait_recv()
        forward_g(d)

    for d in near_first(ny):
        ud[d].wait_recv()
    ue = {}
    for d in near_first(nx):
        ue[d] = go(uband.at[h, :, x], uband.at[h, :, x], "ue", d, to_x(d))

    for e in range(1, nz):
        copy(zsend.at[0], zrecv.at[z], "zs", 0, to_z(1), rk=e).wait_recv()
    acc = zrecv[0].astype(F32)
    for k in range(1, nz):
        acc = acc + zrecv[k].astype(F32)
    sol[...] = acc.reshape(nx * depth, 2 * rank).astype(BF)

    pc, zc = {}, {}

    def partial_core(d):
        p = (y - d) % ny
        for dx in near_first(nx):
            gx[d, dx].wait_recv()
        y_rows = jnp.concatenate([yg[k, p].astype(F32) for k in range(nx)], axis=0).astype(BF)
        part = cross_rows(sol[...], y_rows)
        low, high = part[:rank], part[rank:]
        pown[d] = jnp.where(h == 0, low, high)
        psend[d] = jnp.where(h == 0, high, low)
        pc[d] = go(psend.at[d], psib.at[d], "pc", d, to_sib)

    def send_core(d):
        p = (y - d) % ny
        e = (p + nz - z) % nz
        pc[d].wait_recv()
        csum = (pown[d] + psib[d]).astype(BF)
        csend[d] = csum
        zc[d] = copy(csend.at[d], crecv.at[z], "zc", d, {"row": row, "col": p}, rk=e)

        @pl.when(e != 0)
        def _():
            zc[d].start()

        @pl.when(e == 0)
        def _():
            crecv[z] = csum

    lag = 2
    for k, d in enumerate(order_y):
        partial_core(d)
        if k >= lag:
            send_core(order_y[k - lag])
    for d in order_y[-lag:]:
        send_core(d)

    for d in near_first(nx):
        ue[d].wait_recv()
    uf = go(uband.at[h], uband.at[h], "uf", 0, to_sib)

    keeps = [
        flag_row((1, rank), lanes < rank_map[own_tile, band_cols[i]]).astype(BF) for i in range(2)
    ]

    def gram(out_ref, at, kept_ref, i, other):
        out_ref[at] = jnp.zeros((2 * rank, 2 * rank), F32)

        def body(k, carry):
            part = pl.ds(pl.multiple_of(k * width, 16), width)
            both = jnp.concatenate([kept_ref[i, part, :] * keeps[i], other(k, part)], axis=1)
            out_ref[at] += cross_rows(both, both)
            return carry

        lax.fori_loop(0, points // width, body, 0)

    load_tu.wait()
    for i in range(2):
        gram(gram_left, (0, i), tu, i, lambda k, part: basis[part, :])
    load_tv.wait()
    uf.wait_recv()
    for i in range(2):
        gram(right, (i,), tv, i, lambda k, part: uband[i, k].reshape(width, rank))

    for e in range(1, nz):
        copy(csend.at[0], crecv.at[z], "zc", 0, to_z(1), rk=e).wait_recv()
    core = crecv[0].astype(F32)
    for k in range(1, nz):
        core = core + crecv[k].astype(F32)

    def times_transposed(first, second):
        return lax.dot_general(
            first, second, (((1,), (1,)), ((), ())), precision=HI, preferred_element_type=F32
        )

    for i in range(2):
        lower = flag_row((1, rank), jnp.broadcast_to(band_cols[i] < own_tile, (1, rank)))
        c = core[:, i * rank:(i + 1) * rank] * lower
        g = right[i, :rank, rank:]
        half = jnp.dot(c, right[i, rank:, rank:], precision=HI, preferred_element_type=F32)
        gram_right[0, i, :rank, :rank] = right[i, :rank, :rank]
        gram_right[0, i, :rank, rank:] = -times_transposed(g, c)
        gram_right[0, i, rank:, :rank] = -times_transposed(c, g)
        gram_right[0, i, rank:, rank:] = times_transposed(half, c)

    for one in started:
        one.wait_send()

    @pl.when(y != z)
    def _():
        ut.wait_send()

    for d in order_y:

        @pl.when(((y - d) % ny + nz - z) % nz != 0)
        def _():
            zs[d].wait_send()
            zc[d].wait_send()


def shards(dims, panel_u, panel_v, linv, trail_u, trail_v, rank_map, tile_of_slot, band_cols):
    ny, nx, nz = dims
    points, rank = panel_u.shape[1:]
    depth, width = linv.shape
    py = width // nx
    _, total = plan(ny, nx, nz)
    vmem = pl.BlockSpec(memory_space=pltpu.VMEM)
    smem = pl.BlockSpec(memory_space=pltpu.SMEM)
    hbm = pl.BlockSpec(memory_space=pl.ANY)
    out = jax.ShapeDtypeStruct((1, 2, 2 * rank, 2 * rank), F32)
    scratch = [
        pltpu.VMEM((points, rank), BF),
        pltpu.VMEM((width, rank), BF),
        pltpu.VMEM((width, 2 * rank), BF),
        pltpu.VMEM((nx, 2, py, rank), BF),
        pltpu.VMEM((nz, py, rank), BF),
        pltpu.VMEM((ny, py, rank), BF),
        pltpu.VMEM((py, rank), BF),
        pltpu.VMEM((nx, py, 2 * rank), BF),
        pltpu.VMEM((nx, 2, py, rank), BF),
        pltpu.VMEM((nz, py, rank), BF),
        pltpu.VMEM((ny, py, rank), BF),
        pltpu.VMEM((py, rank), BF),
        pltpu.VMEM((2, nz, nx, py, rank), BF),
        pltpu.VMEM((2, points, rank), BF),
        pltpu.VMEM((2, points, rank), BF),
        pltpu.VMEM((ny, nx, depth, width), BF),
        pltpu.VMEM((ny, nx, depth, 2 * rank), BF),
        pltpu.VMEM((nz, nx, depth, 2 * rank), BF),
        pltpu.VMEM((nx * depth, 2 * rank), BF),
        pltpu.VMEM((nz, depth, 2 * rank), BF),
        pltpu.VMEM((nz, depth, 2 * rank), BF),
        pltpu.VMEM((nx, ny, depth, 2 * rank), BF),
        pltpu.VMEM((nz, 8, rank), jnp.int32),
        pltpu.VMEM((ny, rank, 2 * rank), F32),
        pltpu.VMEM((ny, rank, 2 * rank), F32),
        pltpu.VMEM((ny, rank, 2 * rank), F32),
        pltpu.VMEM((ny, rank, 2 * rank), BF),
        pltpu.VMEM((nz, rank, 2 * rank), BF),
        pltpu.VMEM((2, 2 * rank, 2 * rank), F32),
        pltpu.SemaphoreType.DMA((total,)),
        pltpu.SemaphoreType.DMA((total,)),
        pltpu.SemaphoreType.DMA((5,)),
    ]
    return pl.pallas_call(
        functools.partial(kernel, dims),
        out_shape=(out, out),
        in_specs=[hbm, hbm, hbm, hbm, hbm, smem, smem, smem],
        out_specs=(vmem, vmem),
        scratch_shapes=scratch,
        compiler_params=pltpu.CompilerParams(
            collective_id=0, has_side_effects=True, vmem_limit_bytes=60 * 2**20
        ),
    )(panel_u, panel_v, linv, trail_u, trail_v, rank_map, tile_of_slot, band_cols)


def solution(mesh):
    nz = mesh.shape["col"]
    ny = nz
    nx = mesh.shape["row"] // (2 * ny)
    return jax.shard_map(
        functools.partial(shards, (ny, nx, nz)),
        mesh=mesh,
        in_specs=(
            P("row", None, None),
            P("row", "col", None),
            P("row", "col"),
            P("row", "col", None, None),
            P("row", "col", None, None),
            P(),
            P(),
            P("col"),
        ),
        out_specs=(P("row", "col", None, None), P("row", "col", None, None)),
        check_vma=False,
    )
```

```python
import functools

import jax
import jax.numpy as jnp
from jax import lax
from jax.experimental import pallas as pl
from jax.experimental.pallas import tpu as pltpu
from jax.sharding import PartitionSpec as P

MESH = pl.DeviceIdType.MESH
BF = jnp.bfloat16
F32 = jnp.float32
HI = lax.Precision.HIGHEST


def near_first(n):
    return sorted(range(1, n), key=lambda d: (min(d, n - d), d))


def cross_rows(first, second):
    return lax.dot_general(first, second, (((0,), (0,)), ((), ())), preferred_element_type=F32)


def flag_row(shape_like, cond):
    return jnp.where(cond, jnp.ones(shape_like, F32), jnp.zeros(shape_like, F32))


def plan(ny, nx, nz):
    counts = dict(
        va=2 * nx, ua=2 * nx, vb=ny, ub=ny, vc=2 * nx, bc=nz, v=1, ly=ny, lx=ny * nx, zs=nz, zy=nz,
        gy=ny, gx=ny * nx, ut=1, ud=ny, ue=nx, uf=1, pc=ny, zc=nz,
    )
    base, total = {}, 0
    for name, count in counts.items():
        base[name] = total
        total += count
    return base, total


def kernel(
    dims,
    panel_u, panel_v, linv, trail_u, trail_v, rank_map, tile_of_slot, band_cols,
    gram_left, gram_right,
    basis, vown, vchip, vx, vsel, vy, vpiece, vband, ux, usel, uy, upiece, uband, tu, tv,
    lbuf, zsend, zrecv, sol, zysend, zyrecv, yg, bcbuf,
    pown, psend, psib, csend, crecv, right,
    ssem, rsem, lsem,
):
    ny, nx, nz = dims
    base, _ = plan(ny, nx, nz)
    points, rank = panel_u.shape[1:]
    depth, width = linv.shape
    py = width // nx
    row = lax.axis_index("row")
    z = lax.axis_index("col")
    y, x, h = row // (2 * nx), (row // 2) % nx, row % 2

    def spot(yy, xx, hh):
        return (yy * nx + xx) * 2 + hh

    def to_y(d):
        return {"row": spot((y + d) % ny, x, h), "col": z}

    def to_x(d, flip=0):
        return {"row": spot(y, (x + d) % nx, (h + flip) % 2), "col": z}

    def to_z(d):
        return {"row": row, "col": (z + d) % nz}

    to_sib = to_x(0, 1)
    to_turned = {"row": spot(z, x, h), "col": y}
    chips = [(0, 1)] + [(d, flip) for d in near_first(nx) for flip in (0, 1)]
    started = []

    def copy(src, dst, name, k, where, rk=None):
        return pltpu.make_async_remote_copy(
            src_ref=src, dst_ref=dst,
            send_sem=ssem.at[base[name] + k],
            recv_sem=rsem.at[base[name] + (k if rk is None else rk)],
            device_id=where, device_id_type=MESH,
        )

    def go(src, dst, name, k, where):
        one = copy(src, dst, name, k, where)
        one.start()
        started.append(one)
        return one

    def load(src, dst, k):
        one = pltpu.make_async_copy(src, dst, lsem.at[k])
        one.start()
        return one

    load_pv = load(panel_v.at[0], vown, 0)
    load_l = load(linv, lbuf.at[y, x], 1)
    load_pu = load(panel_u.at[0], basis, 2)

    barrier = pltpu.get_barrier_semaphore()
    peers = [to_y(d) for d in near_first(ny)] + [to_x(d, flip) for d, flip in chips]
    peers += [to_z(d) for d in near_first(nz)]
    for peer in peers:
        pl.semaphore_signal(barrier, inc=1, device_id=peer, device_id_type=MESH)

    @pl.when(y != z)
    def _():
        pl.semaphore_signal(barrier, inc=1, device_id=to_turned, device_id_type=MESH)

    load_tu = load(trail_u.at[0], tu, 3)
    load_tv = load(trail_v.at[0], tv, 4)

    lanes = lax.broadcasted_iota(jnp.int32, (1, rank), 1)
    own_tile = tile_of_slot[row]
    own_mask = flag_row((1, rank), lanes < rank_map[own_tile, own_tile]).astype(BF)
    mine = pl.multiple_of(h * rank, rank)
    odd = lax.broadcasted_iota(jnp.int32, (8, rank), 0) % 2
    bcbuf[z] = jnp.where(odd == 1, band_cols[1], band_cols[0])
    load_pv.wait()
    masked_v = vown[...] * own_mask
    vown[...] = masked_v
    vchip[:, pl.ds(mine, rank)] = masked_v
    load_pu.wait()
    step = points // 4
    for k in range(4):
        part = slice(k * step, (k + 1) * step)
        basis[part, :] = basis[part, :] * own_mask
    load_l.wait()

    pl.semaphore_wait(barrier, len(peers) + jnp.where(y != z, 1, 0))

    def quarter(k):
        return pl.ds(pl.multiple_of(k * py, 16), py)

    def uquarter(k):
        return pl.ds(pl.multiple_of(z * width + k * py, 16), py)

    va, ua, ly, bcs = {}, {}, {}, {}
    for d, flip in chips:
        xx = (x + d) % nx
        va[d, flip] = go(vown.at[quarter(xx), :], vx.at[x, h], "va", 2 * d + flip, to_x(d, flip))
    for d in near_first(nz):
        bcs[d] = go(bcbuf.at[z], bcbuf.at[z], "bc", d, to_z(d))
    for d in near_first(ny):
        ly[d] = go(lbuf.at[y, x], lbuf.at[y, x], "ly", d, to_y(d))
    cv = go(vchip.at[:, pl.ds(mine, rank)], vchip.at[:, pl.ds(mine, rank)], "v", 0, to_sib)
    for d, flip in chips:
        xx = (x + d) % nx
        ua[d, flip] = go(basis.at[uquarter(xx), :], ux.at[x, h], "ua", 2 * d + flip, to_x(d, flip))
    vx[x, h] = vown[quarter(x), :]
    ux[x, h] = basis[uquarter(x), :]

    lx = {}

    def forward_l(d):
        yy = (y - d) % ny
        for dx in near_first(nx):
            lx[d, dx] = go(lbuf.at[yy, x], lbuf.at[yy, x], "lx", d * nx + dx, to_x(dx))

    order_y = [0] + near_first(ny)
    forward_l(0)

    def pick(from_ref, to_ref):
        blocks = [from_ref[k // 2, k % 2] for k in range(2 * nx)]
        for p in range(nz):
            name_row = bcbuf[p, pl.ds(h, 1), :]
            got = jnp.zeros((py, rank), BF)
            for k in range(2 * nx):
                got = got + blocks[k] * flag_row((1, rank), name_row == tiles[k]).astype(BF)
            to_ref[p] = got

    def summed(ref, count):
        total = ref[0]
        for k in range(1, count):
            total = total + ref[k]
        return total

    tiles = [tile_of_slot[spot(y, k // 2, k % 2)] for k in range(2 * nx)]
    for d in near_first(nz):
        bcs[d].wait_recv()
    for one in va.values():
        one.wait_recv()
    pick(vx, vsel)
    vb = {}
    for d in near_first(ny):
        vb[d] = go(vsel.at[(y + d) % ny], vy.at[y], "vb", d, to_y(d))
    vy[y] = vsel[y]

    for d in near_first(ny):
        ly[d].wait_recv()
        forward_l(d)

    for d in near_first(ny):
        vb[d].wait_recv()
    piece = summed(vy, ny)
    vpiece[...] = piece
    vband[x, :, pl.ds(mine, rank)] = piece
    vc = {}
    for d, flip in chips:
        vc[d, flip] = go(
            vpiece, vband.at[x, :, pl.ds(mine, rank)], "vc", 2 * d + flip, to_x(d, flip)
        )

    for one in ua.values():
        one.wait_recv()
    pick(ux, usel)
    ub = {}
    for d in near_first(ny):
        ub[d] = go(usel.at[(y + d) % ny], uy.at[y], "ub", d, to_y(d))
    uy[y] = usel[y]

    for one in vc.values():
        one.wait_recv()
    rows = jnp.concatenate([lbuf[k, x].astype(F32) for k in range(ny)], axis=0).astype(BF)
    part = jnp.dot(rows, vband[...].reshape(width, 2 * rank), preferred_element_type=F32)
    zysend[...] = part.reshape(ny, depth, 2 * rank).astype(BF)
    zy = {}
    for e in near_first(nz):
        zy[e] = go(zysend.at[(z + e) % nz], zyrecv.at[z], "zy", e, to_z(e))
    zyrecv[z] = zysend[z]

    cv.wait_recv()
    zs = {}
    for d in order_y:
        yy = (y - d) % ny
        for dx in near_first(nx):
            lx[d, dx].wait_recv()
        block = lbuf[yy].astype(F32).reshape(nx * depth, width).astype(BF)
        part = jnp.dot(block, vchip[...], preferred_element_type=F32)
        part = part.reshape(nx, depth, 2 * rank).astype(BF)
        zsend[d] = part
        e = (yy + nz - z) % nz
        zs[d] = copy(zsend.at[d], zrecv.at[z], "zs", d, {"row": row, "col": yy}, rk=e)

        @pl.when(e != 0)
        def _():
            zs[d].start()

        @pl.when(e == 0)
        def _():
            zrecv[z] = part

    for d in near_first(ny):
        ub[d].wait_recv()
    piece = summed(uy, ny)
    upiece[...] = piece
    ut = copy(upiece, uband.at[h, z, x], "ut", 0, to_turned)

    @pl.when(y != z)
    def _():
        ut.start()

    @pl.when(y == z)
    def _():
        uband[h, z, x] = piece

    for e in near_first(nz):
        zy[e].wait_recv()
    acc = zyrecv[0].astype(F32)
    for k in range(1, nz):
        acc = acc + zyrecv[k].astype(F32)
    yg[x, y] = acc.astype(BF)
    gy, gx = {}, {}
    for d in near_first(ny):
        gy[d] = go(yg.at[x, y], yg.at[x, y], "gy", d, to_y(d))

    def forward_g(d):
        yy = (y - d) % ny
        for dx in near_first(nx):
            gx[d, dx] = go(yg.at[x, yy], yg.at[x, yy], "gx", d * nx + dx, to_x(dx))

    forward_g(0)

    @pl.when(y != z)
    def _():
        ut.wait_recv()

    ud = {}
    for d in near_first(ny):
        ud[d] = go(uband.at[h, y, x], uband.at[h, y, x], "ud", d, to_y(d))

    for d in near_first(ny):
        gy[d].wait_recv()
        forward_g(d)

    for d in near_first(ny):
        ud[d].wait_recv()
    ue = {}
    for d in near_first(nx):
        ue[d] = go(uband.at[h, :, x], uband.at[h, :, x], "ue", d, to_x(d))

    for e in range(1, nz):
        copy(zsend.at[0], zrecv.at[z], "zs", 0, to_z(1), rk=e).wait_recv()
    acc = zrecv[0].astype(F32)
    for k in range(1, nz):
        acc = acc + zrecv[k].astype(F32)
    sol[...] = acc.reshape(nx * depth, 2 * rank).astype(BF)

    pc, zc = {}, {}

    def partial_core(d):
        p = (y - d) % ny
        for dx in near_first(nx):
            gx[d, dx].wait_recv()
        y_rows = jnp.concatenate([yg[k, p].astype(F32) for k in range(nx)], axis=0).astype(BF)
        part = cross_rows(sol[...], y_rows)
        low, high = part[:rank], part[rank:]
        pown[d] = jnp.where(h == 0, low, high)
        psend[d] = jnp.where(h == 0, high, low)
        pc[d] = go(psend.at[d], psib.at[d], "pc", d, to_sib)

    def send_core(d):
        p = (y - d) % ny
        e = (p + nz - z) % nz
        pc[d].wait_recv()
        csum = (pown[d] + psib[d]).astype(BF)
        csend[d] = csum
        zc[d] = copy(csend.at[d], crecv.at[z], "zc", d, {"row": row, "col": p}, rk=e)

        @pl.when(e != 0)
        def _():
            zc[d].start()

        @pl.when(e == 0)
        def _():
            crecv[z] = csum

    lag = 2
    for k, d in enumerate(order_y):
        partial_core(d)
        if k >= lag:
            send_core(order_y[k - lag])
    for d in order_y[-lag:]:
        send_core(d)

    for d in near_first(nx):
        ue[d].wait_recv()
    uf = go(uband.at[h], uband.at[h], "uf", 0, to_sib)

    def gram(out_ref, at, kept_ref, i, other):
        out_ref[at] = jnp.zeros((2 * rank, 2 * rank), F32)
        keep = flag_row((1, rank), lanes < rank_map[own_tile, band_cols[i]]).astype(BF)

        def body(k, carry):
            part = pl.ds(pl.multiple_of(k * width, 16), width)
            both = jnp.concatenate([kept_ref[i, part, :] * keep, other(k, part)], axis=1)
            out_ref[at] += cross_rows(both, both)
            return carry

        lax.fori_loop(0, points // width, body, 0)

    load_tu.wait()
    for i in range(2):
        gram(gram_left, (0, i), tu, i, lambda k, part: basis[part, :])
    load_tv.wait()
    gram(right, (h,), tv, h, lambda k, part: uband[h, k].reshape(width, rank))
    uf.wait_recv()
    other = 1 - h
    gram(right, (other,), tv, other, lambda k, part: uband[other, k].reshape(width, rank))

    for e in range(1, nz):
        copy(csend.at[0], crecv.at[z], "zc", 0, to_z(1), rk=e).wait_recv()
    core = crecv[0].astype(F32)
    for k in range(1, nz):
        core = core + crecv[k].astype(F32)

    def times_transposed(first, second):
        return lax.dot_general(
            first, second, (((1,), (1,)), ((), ())), precision=HI, preferred_element_type=F32
        )

    for i in range(2):
        lower = flag_row((1, rank), jnp.broadcast_to(band_cols[i] < own_tile, (1, rank)))
        c = core[:, i * rank:(i + 1) * rank] * lower
        g = right[i, :rank, rank:]
        half = jnp.dot(c, right[i, rank:, rank:], precision=HI, preferred_element_type=F32)
        gram_right[0, i, :rank, :rank] = right[i, :rank, :rank]
        gram_right[0, i, :rank, rank:] = -times_transposed(g, c)
        gram_right[0, i, rank:, :rank] = -times_transposed(c, g)
        gram_right[0, i, rank:, rank:] = times_transposed(half, c)

    for one in started:
        one.wait_send()

    @pl.when(y != z)
    def _():
        ut.wait_send()

    for d in order_y:

        @pl.when(((y - d) % ny + nz - z) % nz != 0)
        def _():
            zs[d].wait_send()
            zc[d].wait_send()


def shards(dims, panel_u, panel_v, linv, trail_u, trail_v, rank_map, tile_of_slot, band_cols):
    ny, nx, nz = dims
    points, rank = panel_u.shape[1:]
    depth, width = linv.shape
    py = width // nx
    _, total = plan(ny, nx, nz)
    vmem = pl.BlockSpec(memory_space=pltpu.VMEM)
    smem = pl.BlockSpec(memory_space=pltpu.SMEM)
    hbm = pl.BlockSpec(memory_space=pl.ANY)
    out = jax.ShapeDtypeStruct((1, 2, 2 * rank, 2 * rank), F32)
    scratch = [
        pltpu.VMEM((points, rank), BF),
        pltpu.VMEM((width, rank), BF),
        pltpu.VMEM((width, 2 * rank), BF),
        pltpu.VMEM((nx, 2, py, rank), BF),
        pltpu.VMEM((nz, py, rank), BF),
        pltpu.VMEM((ny, py, rank), BF),
        pltpu.VMEM((py, rank), BF),
        pltpu.VMEM((nx, py, 2 * rank), BF),
        pltpu.VMEM((nx, 2, py, rank), BF),
        pltpu.VMEM((nz, py, rank), BF),
        pltpu.VMEM((ny, py, rank), BF),
        pltpu.VMEM((py, rank), BF),
        pltpu.VMEM((2, nz, nx, py, rank), BF),
        pltpu.VMEM((2, points, rank), BF),
        pltpu.VMEM((2, points, rank), BF),
        pltpu.VMEM((ny, nx, depth, width), BF),
        pltpu.VMEM((ny, nx, depth, 2 * rank), BF),
        pltpu.VMEM((nz, nx, depth, 2 * rank), BF),
        pltpu.VMEM((nx * depth, 2 * rank), BF),
        pltpu.VMEM((nz, depth, 2 * rank), BF),
        pltpu.VMEM((nz, depth, 2 * rank), BF),
        pltpu.VMEM((nx, ny, depth, 2 * rank), BF),
        pltpu.VMEM((nz, 8, rank), jnp.int32),
        pltpu.VMEM((ny, rank, 2 * rank), F32),
        pltpu.VMEM((ny, rank, 2 * rank), F32),
        pltpu.VMEM((ny, rank, 2 * rank), F32),
        pltpu.VMEM((ny, rank, 2 * rank), BF),
        pltpu.VMEM((nz, rank, 2 * rank), BF),
        pltpu.VMEM((2, 2 * rank, 2 * rank), F32),
        pltpu.SemaphoreType.DMA((total,)),
        pltpu.SemaphoreType.DMA((total,)),
        pltpu.SemaphoreType.DMA((5,)),
    ]
    return pl.pallas_call(
        functools.partial(kernel, dims),
        out_shape=(out, out),
        in_specs=[hbm, hbm, hbm, hbm, hbm, smem, smem, smem],
        out_specs=(vmem, vmem),
        scratch_shapes=scratch,
        compiler_params=pltpu.CompilerParams(
            collective_id=0, has_side_effects=True, vmem_limit_bytes=60 * 2**20
        ),
    )(panel_u, panel_v, linv, trail_u, trail_v, rank_map, tile_of_slot, band_cols)


def solution(mesh):
    nz = mesh.shape["col"]
    ny = nz
    nx = mesh.shape["row"] // (2 * ny)
    return jax.shard_map(
        functools.partial(shards, (ny, nx, nz)),
        mesh=mesh,
        in_specs=(
            P("row", None, None),
            P("row", "col", None),
            P("row", "col"),
            P("row", "col", None, None),
            P("row", "col", None, None),
            P(),
            P(),
            P("col"),
        ),
        out_specs=(P("row", "col", None, None), P("row", "col", None, None)),
        check_vma=False,
    )
```

```python
import functools

import jax
import jax.numpy as jnp
from jax import lax
from jax.experimental import pallas as pl
from jax.experimental.pallas import tpu as pltpu
from jax.sharding import PartitionSpec as P

MESH = pl.DeviceIdType.MESH
BF = jnp.bfloat16
F32 = jnp.float32
HI = lax.Precision.HIGHEST


def near_first(n):
    return sorted(range(1, n), key=lambda d: (min(d, n - d), d))


def cross_rows(first, second):
    return lax.dot_general(first, second, (((0,), (0,)), ((), ())), preferred_element_type=F32)


def flag_row(shape_like, cond):
    return jnp.where(cond, jnp.ones(shape_like, F32), jnp.zeros(shape_like, F32))


def plan(ny, nx, nz):
    counts = dict(
        va=2 * nx, ua=2 * nx, vb=ny, ub=ny, vc=2 * nx, bc=nz, v=1, ly=ny, lx=ny * nx, zs=nz, zy=nz,
        gy=ny, gx=ny * nx, ut=1, ud=ny, ue=nx, uf=1, pc=ny, zc=nz,
    )
    base, total = {}, 0
    for name, count in counts.items():
        base[name] = total
        total += count
    return base, total


def kernel(
    dims,
    panel_u, panel_v, linv, trail_u, trail_v, rank_map, tile_of_slot, band_cols,
    gram_left, gram_right,
    basis, vown, vchip, vx, vsel, vy, vpiece, vband, ux, usel, uy, upiece, uband, tu, tv,
    lbuf, zsend, zrecv, sol, zysend, zyrecv, yg, bcbuf,
    pown, psend, psib, csend, crecv, right,
    ssem, rsem, lsem,
):
    ny, nx, nz = dims
    base, _ = plan(ny, nx, nz)
    points, rank = panel_u.shape[1:]
    depth, width = linv.shape
    py = width // nx
    row = lax.axis_index("row")
    z = lax.axis_index("col")
    y, x, h = row // (2 * nx), (row // 2) % nx, row % 2

    def spot(yy, xx, hh):
        return (yy * nx + xx) * 2 + hh

    def to_y(d):
        return {"row": spot((y + d) % ny, x, h), "col": z}

    def to_x(d, flip=0):
        return {"row": spot(y, (x + d) % nx, (h + flip) % 2), "col": z}

    def to_z(d):
        return {"row": row, "col": (z + d) % nz}

    to_sib = to_x(0, 1)
    to_turned = {"row": spot(z, x, h), "col": y}
    chips = [(0, 1)] + [(d, flip) for d in near_first(nx) for flip in (0, 1)]
    started = []

    def copy(src, dst, name, k, where, rk=None):
        return pltpu.make_async_remote_copy(
            src_ref=src, dst_ref=dst,
            send_sem=ssem.at[base[name] + k],
            recv_sem=rsem.at[base[name] + (k if rk is None else rk)],
            device_id=where, device_id_type=MESH,
        )

    def go(src, dst, name, k, where):
        one = copy(src, dst, name, k, where)
        one.start()
        started.append(one)
        return one

    def load(src, dst, k):
        one = pltpu.make_async_copy(src, dst, lsem.at[k])
        one.start()
        return one

    load_pv = load(panel_v.at[0], vown, 0)
    load_l = load(linv, lbuf.at[y, x], 1)
    load_pu = load(panel_u.at[0], basis, 2)

    barrier = pltpu.get_barrier_semaphore()
    peers = [to_y(d) for d in near_first(ny)] + [to_x(d, flip) for d, flip in chips]
    peers += [to_z(d) for d in near_first(nz)]
    for peer in peers:
        pl.semaphore_signal(barrier, inc=1, device_id=peer, device_id_type=MESH)

    @pl.when(y != z)
    def _():
        pl.semaphore_signal(barrier, inc=1, device_id=to_turned, device_id_type=MESH)

    load_tu = load(trail_u.at[0], tu, 3)
    load_tv = load(trail_v.at[0], tv, 4)

    lanes = lax.broadcasted_iota(jnp.int32, (1, rank), 1)
    own_tile = tile_of_slot[row]
    own_mask = flag_row((1, rank), lanes < rank_map[own_tile, own_tile]).astype(BF)
    mine = pl.multiple_of(h * rank, rank)
    odd = lax.broadcasted_iota(jnp.int32, (8, rank), 0) % 2
    bcbuf[z] = jnp.where(odd == 1, band_cols[1], band_cols[0])
    load_pv.wait()
    masked_v = vown[...] * own_mask
    vown[...] = masked_v
    vchip[:, pl.ds(mine, rank)] = masked_v
    load_pu.wait()
    step = points // 4
    for k in range(4):
        part = slice(k * step, (k + 1) * step)
        basis[part, :] = basis[part, :] * own_mask
    load_l.wait()

    pl.semaphore_wait(barrier, len(peers) + jnp.where(y != z, 1, 0))

    def quarter(k):
        return pl.ds(pl.multiple_of(k * py, 16), py)

    def uquarter(k):
        return pl.ds(pl.multiple_of(z * width + k * py, 16), py)

    va, ua, ly, bcs = {}, {}, {}, {}
    for d, flip in chips:
        xx = (x + d) % nx
        va[d, flip] = go(vown.at[quarter(xx), :], vx.at[x, h], "va", 2 * d + flip, to_x(d, flip))
    for d in near_first(nz):
        bcs[d] = go(bcbuf.at[z], bcbuf.at[z], "bc", d, to_z(d))
    for d in near_first(ny):
        ly[d] = go(lbuf.at[y, x], lbuf.at[y, x], "ly", d, to_y(d))
    cv = go(vchip.at[:, pl.ds(mine, rank)], vchip.at[:, pl.ds(mine, rank)], "v", 0, to_sib)
    for d, flip in chips:
        xx = (x + d) % nx
        ua[d, flip] = go(basis.at[uquarter(xx), :], ux.at[x, h], "ua", 2 * d + flip, to_x(d, flip))
    vx[x, h] = vown[quarter(x), :]
    ux[x, h] = basis[uquarter(x), :]

    lx = {}

    def forward_l(d):
        yy = (y - d) % ny
        for dx in near_first(nx):
            lx[d, dx] = go(lbuf.at[yy, x], lbuf.at[yy, x], "lx", d * nx + dx, to_x(dx))

    order_y = [0] + near_first(ny)
    forward_l(0)

    def pick(from_ref, to_ref):
        blocks = [from_ref[k // 2, k % 2] for k in range(2 * nx)]
        for p in range(nz):
            name_row = bcbuf[p, pl.ds(h, 1), :]
            got = jnp.zeros((py, rank), BF)
            for k in range(2 * nx):
                got = got + blocks[k] * flag_row((1, rank), name_row == tiles[k]).astype(BF)
            to_ref[p] = got

    def summed(ref, count):
        total = ref[0]
        for k in range(1, count):
            total = total + ref[k]
        return total

    tiles = [tile_of_slot[spot(y, k // 2, k % 2)] for k in range(2 * nx)]
    for d in near_first(nz):
        bcs[d].wait_recv()
    for one in va.values():
        one.wait_recv()
    pick(vx, vsel)
    vb = {}
    for d in near_first(ny):
        vb[d] = go(vsel.at[(y + d) % ny], vy.at[y], "vb", d, to_y(d))
    vy[y] = vsel[y]

    for d in near_first(ny):
        vb[d].wait_recv()
    piece = summed(vy, ny)
    vpiece[...] = piece
    vband[x, :, pl.ds(mine, rank)] = piece
    vc = {}
    for d, flip in chips:
        vc[d, flip] = go(
            vpiece, vband.at[x, :, pl.ds(mine, rank)], "vc", 2 * d + flip, to_x(d, flip)
        )

    for d in near_first(ny):
        ly[d].wait_recv()
        forward_l(d)

    for one in ua.values():
        one.wait_recv()
    pick(ux, usel)
    ub = {}
    for d in near_first(ny):
        ub[d] = go(usel.at[(y + d) % ny], uy.at[y], "ub", d, to_y(d))
    uy[y] = usel[y]

    for one in vc.values():
        one.wait_recv()
    rows = jnp.concatenate([lbuf[k, x].astype(F32) for k in range(ny)], axis=0).astype(BF)
    part = jnp.dot(rows, vband[...].reshape(width, 2 * rank), preferred_element_type=F32)
    zysend[...] = part.reshape(ny, depth, 2 * rank).astype(BF)
    zy = {}
    for e in near_first(nz):
        zy[e] = go(zysend.at[(z + e) % nz], zyrecv.at[z], "zy", e, to_z(e))
    zyrecv[z] = zysend[z]

    cv.wait_recv()
    zs = {}
    for d in order_y:
        yy = (y - d) % ny
        for dx in near_first(nx):
            lx[d, dx].wait_recv()
        block = lbuf[yy].astype(F32).reshape(nx * depth, width).astype(BF)
        part = jnp.dot(block, vchip[...], preferred_element_type=F32)
        part = part.reshape(nx, depth, 2 * rank).astype(BF)
        zsend[d] = part
        e = (yy + nz - z) % nz
        zs[d] = copy(zsend.at[d], zrecv.at[z], "zs", d, {"row": row, "col": yy}, rk=e)

        @pl.when(e != 0)
        def _():
            zs[d].start()

        @pl.when(e == 0)
        def _():
            zrecv[z] = part

    for d in near_first(ny):
        ub[d].wait_recv()
    piece = summed(uy, ny)
    upiece[...] = piece
    ut = copy(upiece, uband.at[h, z, x], "ut", 0, to_turned)

    @pl.when(y != z)
    def _():
        ut.start()

    @pl.when(y == z)
    def _():
        uband[h, z, x] = piece

    for e in near_first(nz):
        zy[e].wait_recv()
    acc = zyrecv[0].astype(F32)
    for k in range(1, nz):
        acc = acc + zyrecv[k].astype(F32)
    yg[x, y] = acc.astype(BF)
    gy, gx = {}, {}
    for d in near_first(ny):
        gy[d] = go(yg.at[x, y], yg.at[x, y], "gy", d, to_y(d))

    def forward_g(d):
        yy = (y - d) % ny
        for dx in near_first(nx):
            gx[d, dx] = go(yg.at[x, yy], yg.at[x, yy], "gx", d * nx + dx, to_x(dx))

    forward_g(0)

    @pl.when(y != z)
    def _():
        ut.wait_recv()

    ud = {}
    for d in near_first(ny):
        ud[d] = go(uband.at[h, y, x], uband.at[h, y, x], "ud", d, to_y(d))

    for d in near_first(ny):
        gy[d].wait_recv()
        forward_g(d)

    for d in near_first(ny):
        ud[d].wait_recv()
    ue = {}
    for d in near_first(nx):
        ue[d] = go(uband.at[h, :, x], uband.at[h, :, x], "ue", d, to_x(d))

    for e in range(1, nz):
        copy(zsend.at[0], zrecv.at[z], "zs", 0, to_z(1), rk=e).wait_recv()
    acc = zrecv[0].astype(F32)
    for k in range(1, nz):
        acc = acc + zrecv[k].astype(F32)
    sol[...] = acc.reshape(nx * depth, 2 * rank).astype(BF)

    pc, zc = {}, {}

    def partial_core(d):
        p = (y - d) % ny
        for dx in near_first(nx):
            gx[d, dx].wait_recv()
        y_rows = jnp.concatenate([yg[k, p].astype(F32) for k in range(nx)], axis=0).astype(BF)
        part = cross_rows(sol[...], y_rows)
        low, high = part[:rank], part[rank:]
        pown[d] = jnp.where(h == 0, low, high)
        psend[d] = jnp.where(h == 0, high, low)
        pc[d] = go(psend.at[d], psib.at[d], "pc", d, to_sib)

    def send_core(d):
        p = (y - d) % ny
        e = (p + nz - z) % nz
        pc[d].wait_recv()
        csum = (pown[d] + psib[d]).astype(BF)
        csend[d] = csum
        zc[d] = copy(csend.at[d], crecv.at[z], "zc", d, {"row": row, "col": p}, rk=e)

        @pl.when(e != 0)
        def _():
            zc[d].start()

        @pl.when(e == 0)
        def _():
            crecv[z] = csum

    lag = 2
    for k, d in enumerate(order_y):
        partial_core(d)
        if k >= lag:
            send_core(order_y[k - lag])
    for d in order_y[-lag:]:
        send_core(d)

    for d in near_first(nx):
        ue[d].wait_recv()
    uf = go(uband.at[h], uband.at[h], "uf", 0, to_sib)

    def gram(out_ref, at, kept_ref, i, other):
        out_ref[at] = jnp.zeros((2 * rank, 2 * rank), F32)
        keep = flag_row((1, rank), lanes < rank_map[own_tile, band_cols[i]]).astype(BF)

        def body(k, carry):
            part = pl.ds(pl.multiple_of(k * width, 16), width)
            both = jnp.concatenate([kept_ref[i, part, :] * keep, other(k, part)], axis=1)
            out_ref[at] += cross_rows(both, both)
            return carry

        lax.fori_loop(0, points // width, body, 0)

    load_tu.wait()
    for i in range(2):
        gram(gram_left, (0, i), tu, i, lambda k, part: basis[part, :])
    load_tv.wait()
    gram(right, (h,), tv, h, lambda k, part: uband[h, k].reshape(width, rank))
    uf.wait_recv()
    other = 1 - h
    gram(right, (other,), tv, other, lambda k, part: uband[other, k].reshape(width, rank))

    for e in range(1, nz):
        copy(csend.at[0], crecv.at[z], "zc", 0, to_z(1), rk=e).wait_recv()
    core = crecv[0].astype(F32)
    for k in range(1, nz):
        core = core + crecv[k].astype(F32)

    def times_transposed(first, second):
        return lax.dot_general(
            first, second, (((1,), (1,)), ((), ())), precision=HI, preferred_element_type=F32
        )

    for i in range(2):
        lower = flag_row((1, rank), jnp.broadcast_to(band_cols[i] < own_tile, (1, rank)))
        c = core[:, i * rank:(i + 1) * rank] * lower
        g = right[i, :rank, rank:]
        half = jnp.dot(c, right[i, rank:, rank:], precision=HI, preferred_element_type=F32)
        gram_right[0, i, :rank, :rank] = right[i, :rank, :rank]
        gram_right[0, i, :rank, rank:] = -times_transposed(g, c)
        gram_right[0, i, rank:, :rank] = -times_transposed(c, g)
        gram_right[0, i, rank:, rank:] = times_transposed(half, c)

    for one in started:
        one.wait_send()

    @pl.when(y != z)
    def _():
        ut.wait_send()

    for d in order_y:

        @pl.when(((y - d) % ny + nz - z) % nz != 0)
        def _():
            zs[d].wait_send()
            zc[d].wait_send()


def shards(dims, panel_u, panel_v, linv, trail_u, trail_v, rank_map, tile_of_slot, band_cols):
    ny, nx, nz = dims
    points, rank = panel_u.shape[1:]
    depth, width = linv.shape
    py = width // nx
    _, total = plan(ny, nx, nz)
    vmem = pl.BlockSpec(memory_space=pltpu.VMEM)
    smem = pl.BlockSpec(memory_space=pltpu.SMEM)
    hbm = pl.BlockSpec(memory_space=pl.ANY)
    out = jax.ShapeDtypeStruct((1, 2, 2 * rank, 2 * rank), F32)
    scratch = [
        pltpu.VMEM((points, rank), BF),
        pltpu.VMEM((width, rank), BF),
        pltpu.VMEM((width, 2 * rank), BF),
        pltpu.VMEM((nx, 2, py, rank), BF),
        pltpu.VMEM((nz, py, rank), BF),
        pltpu.VMEM((ny, py, rank), BF),
        pltpu.VMEM((py, rank), BF),
        pltpu.VMEM((nx, py, 2 * rank), BF),
        pltpu.VMEM((nx, 2, py, rank), BF),
        pltpu.VMEM((nz, py, rank), BF),
        pltpu.VMEM((ny, py, rank), BF),
        pltpu.VMEM((py, rank), BF),
        pltpu.VMEM((2, nz, nx, py, rank), BF),
        pltpu.VMEM((2, points, rank), BF),
        pltpu.VMEM((2, points, rank), BF),
        pltpu.VMEM((ny, nx, depth, width), BF),
        pltpu.VMEM((ny, nx, depth, 2 * rank), BF),
        pltpu.VMEM((nz, nx, depth, 2 * rank), BF),
        pltpu.VMEM((nx * depth, 2 * rank), BF),
        pltpu.VMEM((nz, depth, 2 * rank), BF),
        pltpu.VMEM((nz, depth, 2 * rank), BF),
        pltpu.VMEM((nx, ny, depth, 2 * rank), BF),
        pltpu.VMEM((nz, 8, rank), jnp.int32),
        pltpu.VMEM((ny, rank, 2 * rank), F32),
        pltpu.VMEM((ny, rank, 2 * rank), F32),
        pltpu.VMEM((ny, rank, 2 * rank), F32),
        pltpu.VMEM((ny, rank, 2 * rank), BF),
        pltpu.VMEM((nz, rank, 2 * rank), BF),
        pltpu.VMEM((2, 2 * rank, 2 * rank), F32),
        pltpu.SemaphoreType.DMA((total,)),
        pltpu.SemaphoreType.DMA((total,)),
        pltpu.SemaphoreType.DMA((5,)),
    ]
    return pl.pallas_call(
        functools.partial(kernel, dims),
        out_shape=(out, out),
        in_specs=[hbm, hbm, hbm, hbm, hbm, smem, smem, smem],
        out_specs=(vmem, vmem),
        scratch_shapes=scratch,
        compiler_params=pltpu.CompilerParams(
            collective_id=0, has_side_effects=True, vmem_limit_bytes=60 * 2**20
        ),
    )(panel_u, panel_v, linv, trail_u, trail_v, rank_map, tile_of_slot, band_cols)


def solution(mesh):
    nz = mesh.shape["col"]
    ny = nz
    nx = mesh.shape["row"] // (2 * ny)
    return jax.shard_map(
        functools.partial(shards, (ny, nx, nz)),
        mesh=mesh,
        in_specs=(
            P("row", None, None),
            P("row", "col", None),
            P("row", "col"),
            P("row", "col", None, None),
            P("row", "col", None, None),
            P(),
            P(),
            P("col"),
        ),
        out_specs=(P("row", "col", None, None), P("row", "col", None, None)),
        check_vma=False,
    )
```
